256 devices in a mesh: dp: 16 (over x, y_lo, core), head: 16 (over z, y_hi).
Axes of the slice: x: 4, y: 4 (y_hi: 2, y_lo: 2; y = y_hi * 2 + y_lo), z: 8, core: 2. Of those that a mesh axis runs over, the one named last changes fastest.
Arguments:
- queries: bfloat16 [32768, 4096], P('dp', 'head'), may hold values from -12 to 12
- keys: bfloat16 [32768, 2048], P('dp', 'head'), may hold values from -12 to 12
- values: bfloat16 [32768, 2048], P('dp', 'head'), may hold values from -6 to 6
- doc_lengths: int32 [16, 16], replicated, may hold values from 0 to 2048, as said below
- out_weight: bfloat16 [4096, 4608], P(None, 'dp'), may hold values from -0.09375 to 0.09375
Outputs:
- mixed: bfloat16 [16, 2048, 4608], P(None, 'head', 'dp')
The draws below stay inside these ranges and needn't reach their ends.
Inputs may be any that keep to these rules, and one draw needn't show every extreme that they name: `doc_lengths`: row r holds the lengths of the documents packed into sequence r in order, each a multiple of 128, summing to 2048, followed by zeros; some row holds a single document of 2048 tokens.
All inputs are finite; a program needn't handle non-finite values.
Results may differ from the reference program's by a relative error of at most 0.014.
Values may be sent and summed in bfloat16 or wider, within the bound.
A program may use at most 128 MiB of HBM per device.

```python
import jax
import jax.numpy as jnp
from jax import lax

D = 4608
QH = 32
KVH = 16
HD = 128
SEQ = 2048
UNIT = 128
REPLICAS = 16
TOKENS = 32768


def draw_doc_lengths(key, part):
    unit_count = SEQ // UNIT
    first_key, second_key, third_key = jax.random.split(key, 3)
    base_flag = jax.random.randint(first_key, (REPLICAS,), 0, 2)
    chosen = jax.random.randint(second_key, (), 0, REPLICAS)
    rows_index = jnp.arange(REPLICAS, dtype=jnp.int32)
    half_count = REPLICAS // 2
    mirrored = jnp.bitwise_xor(rows_index, half_count)
    heavy_flag = jnp.where(rows_index < half_count, base_flag, 1 - base_flag[mirrored])
    cut_odds = jnp.where(heavy_flag == 1, 8, 75)
    cut_draw = jax.random.randint(third_key, (REPLICAS, unit_count - 1), 0, 100)
    cut_flags = (cut_draw < cut_odds[:, None]).astype(jnp.int32)
    partner = jnp.bitwise_xor(chosen, half_count)
    cut_flags = jnp.where((rows_index == chosen)[:, None], 0, cut_flags)
    cut_flags = jnp.where((rows_index == partner)[:, None], 1, cut_flags)
    closing = jnp.concatenate([cut_flags, jnp.ones((REPLICAS, 1), jnp.int32)], axis=1)
    doc_number = jnp.cumsum(closing, axis=1).astype(jnp.int32) - closing
    slots = jnp.arange(unit_count, dtype=jnp.int32)
    counts = jnp.sum((doc_number[:, :, None] == slots[None, None, :]).astype(jnp.int32), axis=1)
    return (counts * UNIT).astype(jnp.int32)


def block_levels(key, shape, cuts, least, largest):
    def one(position, shards_of):
        draws = jax.random.uniform(jax.random.fold_in(jax.random.fold_in(key, 6), position), (shards_of,), jnp.float32, least / len(cuts), largest / len(cuts))
        return jnp.repeat(jnp.exp(draws), shape[position] // shards_of).reshape((-1,) + (1,) * (len(shape) - position - 1))

    factor_of = one(*cuts[0])
    for cut in cuts[1:]:
        factor_of = factor_of * one(*cut)
    return factor_of


def gaussian(own_key, extent, width, most, cuts=(), held_as=jnp.bfloat16):
    values = width * jax.random.normal(own_key, extent, jnp.float32)
    if cuts:
        values = values * block_levels(own_key, extent, cuts, -0.22, 0.18)
    return jnp.clip(values, -most, most).astype(held_as)


def setup_inputs(seed: int = 0) -> dict:
    arg_keys = jax.random.split(jax.random.key(seed), 6)
    queries = gaussian(arg_keys[0], (TOKENS, QH * HD), 2.0, 12.0, ((0, 16), (1, 16)))
    keys = gaussian(arg_keys[1], (TOKENS, KVH * HD), 2.0, 12.0, ((0, 16), (1, 16)))
    values = gaussian(arg_keys[2], (TOKENS, KVH * HD), 1.0, 6.0, ((0, 16), (1, 16)))
    doc_lengths = draw_doc_lengths(jax.random.fold_in(arg_keys[5], 71), 0)
    out_weight = gaussian(arg_keys[4], (QH * HD, D), (QH * HD) ** -0.5, 0.09375, ((1, 16),))
    return dict(queries=queries, keys=keys, values=values, doc_lengths=doc_lengths, out_weight=out_weight)


query_scale = 1.0 / 12.0
soft_cap = 50.0


def reference(queries, keys, values, doc_lengths, out_weight):
    group_size = QH // KVH
    doc_ends = jnp.cumsum(doc_lengths, axis=1).astype(jnp.int32)
    positions = jnp.arange(SEQ, dtype=jnp.int32)
    doc_of = jnp.sum((doc_ends[:, None, :] <= positions[None, :, None]).astype(jnp.int32), axis=2).astype(jnp.int32)
    query_heads = queries.reshape(REPLICAS, SEQ, KVH, group_size, HD).transpose(0, 2, 1, 3, 4).reshape(REPLICAS * KVH, SEQ, group_size, HD)
    key_heads = keys.reshape(REPLICAS, SEQ, KVH, HD).transpose(0, 2, 1, 3).reshape(REPLICAS * KVH, SEQ, HD)
    value_heads = values.reshape(REPLICAS, SEQ, KVH, HD).transpose(0, 2, 1, 3).reshape(REPLICAS * KVH, SEQ, HD)
    doc_items = jnp.repeat(doc_of, KVH, axis=0)
    causal = positions[:, None] >= positions[None, :]

    def one_head(item):
        q_item, k_item, v_item, d_item = item
        raw_score = jnp.einsum("qgd,pd->gqp", q_item.astype(jnp.float32), k_item.astype(jnp.float32))
        capped = soft_cap * jnp.tanh(raw_score * query_scale / soft_cap)
        allowed = (d_item[:, None] == d_item[None, :]) & causal
        weight = jnp.where(allowed[None], jnp.exp(capped), jnp.float32(0.0)).astype(jnp.bfloat16)
        numerator = jnp.einsum("gqp,pd->qgd", weight.astype(jnp.float32), v_item.astype(jnp.float32))
        denominator = jnp.sum(weight.astype(jnp.float32), axis=2).T
        return (numerator / denominator[:, :, None]).astype(jnp.bfloat16)

    attended = lax.map(one_head, (query_heads, key_heads, value_heads, doc_items))
    attended = attended.reshape(REPLICAS, KVH, SEQ, group_size, HD).transpose(0, 2, 1, 3, 4).reshape(REPLICAS * SEQ, QH * HD)
    mixed = jnp.dot(attended, out_weight, preferred_element_type=jnp.float32).astype(jnp.bfloat16)
    return mixed.reshape(REPLICAS, SEQ, D)
```

```python
import math

import jax
import jax.numpy as jnp
from jax import lax
from jax.experimental import pallas as pl
from jax.experimental.pallas import tpu as pltpu
from jax.sharding import PartitionSpec as P

HD = 128
BLK = 128
SEQ = 2048
STEPS = 8
CHUNK = 256
FEAT = 288
MAIN = 256
REM = FEAT - MAIN
HEADS = 16
DEPTH = 4096
OROWS = BLK + 16
SCALE = 1.0 / 12.0 / 50.0
GAIN = 50.0 * math.log2(math.e)
MESH = pl.DeviceIdType.MESH
F32 = jnp.float32
BF16 = jnp.bfloat16


def lane_group(rows):
    return lax.broadcasted_iota(jnp.int32, (rows, 128), 1) // REM


def merge_lanes(parts, group):
    out = parts[0]
    for g in range(1, 4):
        out = jnp.where(group == g, parts[g], out)
    return out


def roll(x, by):
    by = by % 128
    return x if by == 0 else pltpu.roll(x, by, 1)


def kernel(
    q_hbm, k_hbm, v_hbm, doc_ref, w_hbm, out_ref,
    q_ref, k_ref, v_ref, w_ref, block_doc,
    acc, stage, gathered, wm, pk, rem_w, acc1, acc2, ostage, obuf,
    ld_sem, a_send, a_recv, x_send, x_recv, f_send, f_recv,
    w_send, w_recv, p_send, p_recv, s_send, s_recv, o_send, o_recv,
):
    dp, head = lax.axis_index("dp"), lax.axis_index("head")
    x, low = dp // 4, lax.rem(dp, 4)
    right = lax.rem(x + 1, 4) * 4 + low
    left = lax.rem(x + 3, 4) * 4 + low
    core_mate = dp + 1 - 2 * lax.rem(dp, 2)
    y_mate = dp + 2 - 4 * lax.rem(dp // 2, 2)
    both_mate = core_mate + 2 - 4 * lax.rem(dp // 2, 2)
    head_mate = head + 1 - 2 * lax.rem(head, 2)
    half = head // 8
    pair = jnp.minimum(head, 15 - head)
    mates = (dp, core_mate, y_mate, both_mate)

    def copy_to(src, dst, send, recv, to_dp, to_head):
        return pltpu.make_async_remote_copy(
            src_ref=src, dst_ref=dst, send_sem=send, recv_sem=recv,
            device_id={"dp": to_dp, "head": to_head}, device_id_type=MESH,
        )

    loads = [
        pltpu.make_async_copy(q_hbm, q_ref, ld_sem.at[0]),
        pltpu.make_async_copy(k_hbm, k_ref, ld_sem.at[1]),
        pltpu.make_async_copy(v_hbm, v_ref, ld_sem.at[2]),
        pltpu.make_async_copy(w_hbm, w_ref, ld_sem.at[3]),
    ]
    for load in loads:
        load.start()
    barrier = pltpu.get_barrier_semaphore()

    def greet(d, to_dp, to_head):
        pl.semaphore_signal(barrier, inc=1, device_id={"dp": to_dp, "head": to_head}, device_id_type=MESH)

    def greet_heads(n, _):
        greet(None, dp, lax.rem(head + n, HEADS))
        return 0

    lax.fori_loop(1, HEADS, greet_heads, 0)
    greet(None, right, head)
    greet(None, left, head)
    greet(None, core_mate, head)
    greet(None, y_mate, head)
    greet(None, both_mate, head)
    greet(None, y_mate, head_mate)

    ends = []
    total = jnp.int32(0)
    for n in range(16):
        total = total + doc_ref[dp, n]
        ends.append(total)

    def number(b, _):
        count = jnp.int32(0)
        for end in ends:
            count = count + jnp.where(end <= b * BLK, 1, 0).astype(jnp.int32)
        block_doc[b] = count
        return 0

    lax.fori_loop(0, 16, number, 0)
    for load in loads[:3]:
        load.wait()
    pl.semaphore_wait(barrier, 21)

    def w_copy(way, n):
        rows = pl.ds(pl.multiple_of(way * 2048 + n * 256, 256), 256)
        return copy_to(
            w_hbm.at[rows, pl.ds(0, MAIN)], wm.at[1, rows], w_send.at[way, n], w_recv.at[way, n],
            y_mate, head if way == 0 else head_mate,
        )

    def p_copy(way):
        rows = pl.ds(way * 512, 512)
        return copy_to(
            pk.at[0, rows], pk.at[2, rows], p_send.at[way], p_recv.at[way],
            y_mate, head if way == 0 else head_mate,
        )

    def core_copy(n):
        if n == 0:
            src, dst = w_hbm.at[:, pl.ds(0, MAIN)], wm.at[0]
        elif n == 1:
            src, dst = pk.at[0], pk.at[1]
        elif n == 2:
            src, dst = wm.at[1], wm.at[2]
        else:
            src, dst = pk.at[2], pk.at[3]
        return copy_to(src, dst, s_send.at[n], s_recv.at[n], core_mate, head)

    def a_copy(t, s, to_head):
        return copy_to(stage.at[t, s], gathered.at[0, t, half], a_send.at[t, s], a_recv.at[t, half], dp, to_head)

    def a_arrival(u, s):
        return copy_to(stage.at[u, s], gathered.at[0, u, s], a_send.at[u, s], a_recv.at[u, s], dp, head)

    def x_copy(way, u):
        return copy_to(
            gathered.at[0, u], gathered.at[1 + way, u], x_send.at[way, u], x_recv.at[way, u],
            right if way == 0 else left, head,
        )

    def f_copy(way, u):
        return copy_to(
            gathered.at[1 + way, u, way], gathered.at[3, u, way], f_send.at[way, u], f_recv.at[way, u],
            right if way == 0 else left, head,
        )

    differences = lax.rem(lax.broadcasted_iota(jnp.int32, (2 * BLK, CHUNK), 0), BLK) - lax.broadcasted_iota(
        jnp.int32, (2 * BLK, CHUNK), 1
    )

    def tile(block, chunk, diagonal):
        rows = pl.ds(pl.multiple_of(block * BLK, BLK), BLK)
        cols = pl.ds(pl.multiple_of(chunk * CHUNK, CHUNK), CHUNK)
        q_two = jnp.concatenate([q_ref[rows, 0:HD], q_ref[rows, HD : 2 * HD]], axis=0)
        raw = lax.dot_general(q_two, k_ref[cols, :], (((1,), (1,)), ((), ())), preferred_element_type=F32)
        weight = jnp.exp2(jnp.tanh(raw * SCALE) * GAIN)
        if diagonal:
            weight = jnp.where(differences >= chunk * CHUNK - block * BLK, weight, 0.0)
        own = block_doc[block]
        live = [
            jnp.full((BLK, HD), jnp.where(block_doc[2 * chunk + n] == own, 1.0, 0.0).astype(F32), F32).astype(BF16)
            for n in range(2)
        ]
        live = jnp.concatenate(live, axis=0)
        value_two = jnp.concatenate([v_ref[cols, :] * live, live], axis=1)
        return jnp.dot(weight.astype(BF16), value_two, preferred_element_type=F32)

    def attend(t):
        j = lax.rem(head + t, 8)
        first = jnp.where(half == 0, j, 15 - j)
        second = 15 - first
        near = first // 2
        acc[0] = tile(first, first // 2, True)
        acc[1] = tile(second, second // 2, True)
        for n in range(7):
            in_first = n < near
            slot = jnp.where(in_first, 0, 1)
            block = jnp.where(in_first, first, second)
            chunk = jnp.where(in_first, n, n - near)
            acc[slot] += tile(block, chunk, False)
        for s, block in enumerate((first, second)):
            both = acc[s]
            result = (both[:, 0:HD] / both[:, HD : 2 * HD]).astype(BF16)
            result = jnp.concatenate([result[0:BLK], result[BLK : 2 * BLK]], axis=1)

            @pl.when(block == head)
            def _():
                gathered[0, t, half] = result

            @pl.when(block != head)
            def _():
                stage[t, s] = result
                a_copy(t, s, block).start()

    def source(u, s):
        return lax.rem(pair - u + 8, 8) + 8 * s

    core_copy(0).start()

    def step(t, _):
        @pl.when(t < STEPS)
        def _():
            w_copy(0, t).start()
            w_copy(1, t).start()
            attend(t)

        @pl.when(jnp.logical_and(t >= 1, t < STEPS + 1))
        def _():
            u = t - 1
            for s in range(2):
                @pl.when(source(u, s) != head)
                def _():
                    a_arrival(u, s).wait_recv()
            x_copy(0, u).start()
            x_copy(1, u).start()

        @pl.when(t >= 2)
        def _():
            u = t - 2
            for way in range(2):
                x_copy(way, u).wait_recv()
                f_copy(way, u).start()

        return 0

    lax.fori_loop(0, STEPS + 2, step, 0)

    loads[3].wait()
    group = lane_group(128)

    def pack(n, _):
        rows = pl.multiple_of(n * 128, 128)
        parts = []
        for g in range(4):
            part = w_ref[pl.ds(g * 1024 + rows, 128), MAIN:FEAT].astype(F32)
            part = jnp.concatenate([part, jnp.zeros((128, 128 - REM), F32)], axis=1)
            parts.append(roll(part, REM * g))
        pk[0, pl.ds(rows, 128), :] = merge_lanes(parts, group).astype(BF16)
        return 0

    lax.fori_loop(0, 8, pack, 0)
    core_copy(1).start()
    p_copy(0).start()
    p_copy(1).start()

    def w_arrive(n, _):
        w_copy(0, n).wait_recv()
        w_copy(1, n).wait_recv()
        return 0

    lax.fori_loop(0, STEPS, w_arrive, 0)
    core_copy(2).start()
    p_copy(0).wait_recv()
    p_copy(1).wait_recv()
    core_copy(3).start()
    for n in (0, 1, 3, 2):
        core_copy(n).wait_recv()

    def spread(n, _):
        rows = pl.multiple_of(n * 128, 128)
        parts = [pk[g, pl.ds(rows, 128), :].astype(F32) for g in range(4)]
        for a in range(4):
            merged = merge_lanes([roll(parts[g], REM * (g - a)) for g in range(4)], group)
            rem_w[pl.ds(a * 1024 + rows, 128), :] = merged.astype(BF16)
        return 0

    lax.fori_loop(0, 8, spread, 0)

    def project(total, lhs_of):
        total[...] = jnp.zeros_like(total)

        def add(u, _):
            parts = [None] * 5
            for s in range(2):
                rows = pl.ds(pl.multiple_of(source(u, s) * 256, 256), 256)
                lhs = lhs_of(u, s)
                for n in range(5):
                    if n == 0:
                        rhs = w_ref[rows, 0:MAIN]
                    elif n == 4:
                        rhs = rem_w[rows, :]
                    else:
                        rhs = wm[n - 1, rows, :]
                    term = jnp.dot(lhs, rhs, preferred_element_type=F32)
                    parts[n] = term if parts[n] is None else parts[n] + term
            for n in range(5):
                cols = pl.ds(n * 256, 256 if n < 4 else 128)
                total[:, cols] += parts[n]
            return 0

        lax.fori_loop(0, STEPS, add, 0)

    small = lane_group(16)
    places = (x, lax.rem(x + 3, 4), lax.rem(x + 1, 4), lax.rem(x + 2, 4))

    def o_copy(n, slot):
        row = places[slot] * 4 + low
        return copy_to(
            ostage.at[n - 1, slot], obuf.at[row], o_send.at[n - 1, slot], o_recv.at[n - 1, slot], mates[n], head
        )

    def o_arrival(n, slot):
        row = places[slot] * 4 + lax.rem(mates[n], 4)
        return copy_to(
            ostage.at[n - 1, slot], obuf.at[row], o_send.at[n - 1, slot], o_recv.at[n - 1, slot], mates[n], head
        )

    def emit(total, base, slot):
        at = base * BLK
        rest = total[at : at + BLK, 1024:1152]
        for n in (2, 3, 1):
            ostage[n - 1, slot, 0:BLK, :] = total[at : at + BLK, n * 256 : (n + 1) * 256].astype(BF16)
            for side in range(2):
                parts = [
                    roll(rest[16 * (4 * side + g) : 16 * (4 * side + g) + 16], REM * (g - n)) for g in range(4)
                ]
                ostage[n - 1, slot, BLK:OROWS, side * 128 : side * 128 + 128] = merge_lanes(parts, small).astype(BF16)
            o_copy(n, slot).start()
        row = places[slot] * 4 + low
        out_ref[row, :, 0:MAIN] = total[at : at + BLK, 0:256].astype(BF16)
        out_ref[row, :, MAIN:FEAT] = rest[:, 0:REM].astype(BF16)

    project(acc1, lambda u, s: gathered[0:3, u, s].reshape(3 * BLK, 256))
    for slot in range(3):
        emit(acc1, slot, slot)

    def f_arrive(u, _):
        f_copy(0, u).wait_recv()
        f_copy(1, u).wait_recv()
        return 0

    lax.fori_loop(0, STEPS, f_arrive, 0)
    project(acc2, lambda u, s: gathered[3, u, s])
    emit(acc2, 0, 3)

    for slot in range(4):
        for n in range(1, 4):
            o_arrival(n, slot).wait_recv()
            row = places[slot] * 4 + lax.rem(mates[n], 4)
            out_ref[row, :, 0:MAIN] = obuf[row, 0:BLK, :]
            for side in range(2):
                packed = obuf[row, BLK:OROWS, side * 128 : side * 128 + 128].astype(F32)
                for g in range(4):
                    at = 16 * (4 * side + g)
                    out_ref[row, at : at + 16, MAIN:FEAT] = roll(packed, -REM * g)[:, 0:REM].astype(BF16)

    def sent(t, _):
        j = lax.rem(head + t, 8)
        first = jnp.where(half == 0, j, 15 - j)
        for s, block in enumerate((first, 15 - first)):
            @pl.when(block != head)
            def _():
                a_copy(t, s, block).wait_send()
        for way in range(2):
            x_copy(way, t).wait_send()
            f_copy(way, t).wait_send()
            w_copy(way, t).wait_send()
        return 0

    lax.fori_loop(0, STEPS, sent, 0)
    for n in range(4):
        core_copy(n).wait_send()
    p_copy(0).wait_send()
    p_copy(1).wait_send()
    for slot in range(4):
        for n in range(1, 4):
            o_copy(n, slot).wait_send()


def body(queries, keys, values, doc_lengths, out_weight):
    dma = pltpu.SemaphoreType.DMA
    anywhere = pl.BlockSpec(memory_space=pl.ANY)
    return pl.pallas_call(
        kernel,
        out_shape=jax.ShapeDtypeStruct((16, BLK, FEAT), BF16),
        in_specs=[anywhere, anywhere, anywhere, pl.BlockSpec(memory_space=pltpu.SMEM), anywhere],
        out_specs=pl.BlockSpec(memory_space=pltpu.VMEM),
        scratch_shapes=[
            pltpu.VMEM((SEQ, 2 * HD), BF16),
            pltpu.VMEM((SEQ, HD), BF16),
            pltpu.VMEM((SEQ, HD), BF16),
            pltpu.VMEM((DEPTH, FEAT), BF16),
            pltpu.SMEM((16,), jnp.int32),
            pltpu.VMEM((2, 2 * BLK, 2 * HD), F32),
            pltpu.VMEM((STEPS, 2, BLK, 256), BF16),
            pltpu.VMEM((4, STEPS, 2, BLK, 256), BF16),
            pltpu.VMEM((3, DEPTH, MAIN), BF16),
            pltpu.VMEM((4, 1024, 128), BF16),
            pltpu.VMEM((DEPTH, 128), BF16),
            pltpu.VMEM((3 * BLK, 1152), F32),
            pltpu.VMEM((BLK, 1152), F32),
            pltpu.VMEM((3, 4, OROWS, 256), BF16),
            pltpu.VMEM((16, OROWS, 256), BF16),
            dma((4,)),
            dma((STEPS, 2)), dma((STEPS, 2)),
            dma((2, STEPS)), dma((2, STEPS)),
            dma((2, STEPS)), dma((2, STEPS)),
            dma((2, STEPS)), dma((2, STEPS)),
            dma((2,)), dma((2,)),
            dma((4,)), dma((4,)),
            dma((3, 4)), dma((3, 4)),
        ],
        compiler_params=pltpu.CompilerParams(
            collective_id=0, has_side_effects=True, vmem_limit_bytes=56 * 1024 * 1024
        ),
    )(queries, keys, values, doc_lengths, out_weight)


def solution(mesh):
    return jax.shard_map(
        body,
        mesh=mesh,
        in_specs=(P("dp", "head"), P("dp", "head"), P("dp", "head"), P(), P(None, "dp")),
        out_specs=P(None, "head", "dp"),
        check_vma=False,
    )
```

```python
import math

import jax
import jax.numpy as jnp
from jax import lax
from jax.experimental import pallas as pl
from jax.experimental.pallas import tpu as pltpu
from jax.sharding import PartitionSpec as P

HD = 128
BLK = 128
SEQ = 2048
CHUNK = 256
FEAT = 288
HEADS = 16
EARLY = 2
LAG_A, LAG_W, LAG_Z, LAG_X = 6, 16, 20, 10
SCALE = 1.0 / 12.0 / 50.0
GAIN = 50.0 * math.log2(math.e)
MESH = pl.DeviceIdType.MESH
F32 = jnp.float32
BF16 = jnp.bfloat16


def kernel(
    q_hbm, k_hbm, v_hbm, doc_ref, w_hbm, out_ref,
    q_ref, k_ref, v_ref, block_doc,
    acc, stage, gathered, wt, total, ostage,
    ld_sem, l_sem, a_send, a_recv, x_send, x_recv, f_send, f_recv,
    w_send, w_recv, z_send, z_recv, s_send, s_recv, m_send, m_recv, o_send, o_recv,
):
    dp, head = lax.axis_index("dp"), lax.axis_index("head")
    x, low = dp // 4, lax.rem(dp, 4)
    z, y_high = head // 2, lax.rem(head, 2)
    odd = lax.rem(z, 2)
    right = lax.rem(x + 1, 4) * 4 + low
    left = lax.rem(x + 3, 4) * 4 + low
    core_mate = dp + 1 - 2 * lax.rem(dp, 2)
    y_mate = dp + 2 - 4 * lax.rem(dp // 2, 2)
    both_mate = core_mate + 2 - 4 * lax.rem(dp // 2, 2)
    head_mate = head + 1 - 2 * y_high
    mates = (dp, core_mate, y_mate, both_mate)

    def copy_to(src, dst, send, recv, to_dp, to_head):
        return pltpu.make_async_remote_copy(
            src_ref=src, dst_ref=dst, send_sem=send, recv_sem=recv,
            device_id={"dp": to_dp, "head": to_head}, device_id_type=MESH,
        )

    def shifted(k, sign):
        far = (k + 2) // 4
        up = jnp.where(lax.rem(k, 2) == 0, far, 8 - far)
        across = jnp.where((far == 0) | (far == 4), lax.rem(k, 2), lax.rem(k // 2 + 1, 2))
        return lax.rem(z + 8 + sign * up, 8) * 2 + lax.rem(y_high + across, 2)

    loads = [
        pltpu.make_async_copy(q_hbm, q_ref, ld_sem.at[0]),
        pltpu.make_async_copy(k_hbm, k_ref, ld_sem.at[1]),
        pltpu.make_async_copy(v_hbm, v_ref, ld_sem.at[2]),
    ]
    for load in loads:
        load.start()

    def w_load(n):
        cols = pl.ds(pl.multiple_of(n * 256, 256), 256)
        return pltpu.make_async_copy(w_hbm.at[:, cols], wt.at[n, pl.ds(0, FEAT)], l_sem.at[n])

    def start_load(n, _):
        w_load(n).start()
        return 0

    lax.fori_loop(0, HEADS, start_load, 0)
    barrier = pltpu.get_barrier_semaphore()

    def greet(to_dp, to_head):
        pl.semaphore_signal(barrier, inc=1, device_id={"dp": to_dp, "head": to_head}, device_id_type=MESH)

    def greet_heads(n, _):
        greet(dp, lax.rem(head + n, HEADS))
        return 0

    lax.fori_loop(1, HEADS, greet_heads, 0)
    greet(right, head)
    greet(left, head)
    greet(core_mate, head)
    greet(y_mate, head)
    greet(both_mate, head)
    greet(y_mate, head_mate)

    ends = []
    end = jnp.int32(0)
    for n in range(16):
        end = end + doc_ref[dp, n]
        ends.append(end)

    def number(b, _):
        count = jnp.int32(0)
        for end in ends:
            count = count + jnp.where(end <= b * BLK, 1, 0).astype(jnp.int32)
        block_doc[b] = count
        return 0

    lax.fori_loop(0, 16, number, 0)
    for load in loads:
        load.wait()

    differences = lax.rem(lax.broadcasted_iota(jnp.int32, (2 * BLK, CHUNK), 0), BLK) - lax.broadcasted_iota(
        jnp.int32, (2 * BLK, CHUNK), 1
    )

    def tile(q_two, block, chunk, diagonal):
        cols = pl.ds(pl.multiple_of(chunk * CHUNK, CHUNK), CHUNK)
        raw = lax.dot_general(q_two, k_ref[cols, :], (((1,), (1,)), ((), ())), preferred_element_type=F32)
        weight = jnp.exp2(jnp.tanh(raw * SCALE) * GAIN)
        if diagonal:
            weight = jnp.where(differences >= chunk * CHUNK - block * BLK, weight, 0.0)
        own = block_doc[block]
        live = []
        for n in range(2):
            on = block_doc[2 * chunk + n] == own
            if not diagonal:
                on = jnp.logical_and(on, chunk < block // 2)
            live.append(jnp.full((BLK, HD), jnp.where(on, 1.0, 0.0).astype(F32), F32).astype(BF16))
        live = jnp.concatenate(live, axis=0)
        value_two = jnp.concatenate([v_ref[cols, :] * live, live], axis=1)
        return jnp.dot(weight.astype(BF16), value_two, preferred_element_type=F32)

    def attend(k, block, into):
        rows = pl.ds(pl.multiple_of(block * BLK, BLK), BLK)

        def tiles(others):
            q_two = jnp.concatenate([q_ref[rows, 0:HD], q_ref[rows, HD : 2 * HD]], axis=0)
            both = tile(q_two, block, block // 2, True)
            for n in range(others):
                both = both + tile(q_two, block, n, False)
            acc[...] = both

        pl.when(block < 8)(lambda: tiles(3))
        pl.when(block >= 8)(lambda: tiles(7))
        both = acc[...]
        result = (both[:, 0:HD] / both[:, HD : 2 * HD]).astype(BF16)
        into[...] = jnp.concatenate([result[0:BLK], result[BLK : 2 * BLK]], axis=1)

    def a_copy(k):
        return copy_to(stage.at[k], gathered.at[0, k], a_send.at[k], a_recv.at[k], dp, shifted(k, 1))

    def x_copy(way, k):
        return copy_to(
            gathered.at[0, k], gathered.at[1 + way, k], x_send.at[way, k], x_recv.at[way, k],
            right if way == 0 else left, head,
        )

    def f_copy(k):
        way = lax.rem(k, 2)
        return copy_to(
            gathered.at[1 + way, k], gathered.at[3, k], f_send.at[k], f_recv.at[k],
            jnp.where(way == 0, right, left), head,
        )

    own_rows, mate_rows, far_rows, both_rows = (pl.ds(n * FEAT, FEAT) for n in range(4))

    def w_copy(n):
        c = 2 * n + odd
        return copy_to(
            wt.at[c, own_rows], wt.at[c, far_rows], w_send.at[n], w_recv.at[n],
            y_mate, jnp.where(lax.rem(n, 2) == 0, head, head_mate),
        )

    def z_copy(n, parity):
        c = 2 * n + parity
        up = jnp.where(lax.rem(n // 2, 2) == 0, 1, 7)
        return copy_to(
            wt.at[c, far_rows], wt.at[c, far_rows], z_send.at[n], z_recv.at[n], dp, lax.rem(z + up, 8) * 2 + y_high
        )

    def s_copy(c):
        return copy_to(wt.at[c, far_rows], wt.at[c, both_rows], s_send.at[c], s_recv.at[c], core_mate, head)

    m_copy = copy_to(wt.at[:, own_rows], wt.at[:, mate_rows], m_send, m_recv, core_mate, head)

    attend(0, head, gathered.at[0, 0])

    def early(k, _):
        attend(k, shifted(k, 1), stage.at[k])
        return 0

    lax.fori_loop(1, EARLY, early, 0)

    def end_load(n, _):
        w_load(n).wait()
        return 0

    lax.fori_loop(0, HEADS, end_load, 0)
    pl.semaphore_wait(barrier, 21)

    def early_send(k, _):
        a_copy(k).start()
        return 0

    lax.fori_loop(1, EARLY, early_send, 0)

    def send_w(n, _):
        w_copy(n).start()
        return 0

    lax.fori_loop(0, 8, send_w, 0)
    m_copy.start()

    def step(t, _):
        @pl.when(t < HEADS)
        def _():
            attend(t, shifted(t, 1), stage.at[t])
            a_copy(t).start()

        def during(lag, count, act):
            k = t - lag
            pl.when(jnp.logical_and(k >= 0, k < count))(lambda: act(k))

        def pass_own(k):
            @pl.when(k > 0)
            def _():
                a_copy(k).wait_recv()
            x_copy(0, k).start()
            x_copy(1, k).start()

        def pass_w(n):
            w_copy(n).wait_recv()
            z_copy(n, odd).start()
            s_copy(2 * n + odd).start()

        def pass_z(n):
            z_copy(n, 1 - odd).wait_recv()
            s_copy(2 * n + 1 - odd).start()

        def pass_far(k):
            x_copy(0, k).wait_recv()
            x_copy(1, k).wait_recv()
            f_copy(k).start()

        during(LAG_A, HEADS, pass_own)
        during(LAG_W, 8, pass_w)
        during(LAG_Z, 8, pass_z)
        during(LAG_X, HEADS, pass_far)
        return 0

    lax.fori_loop(EARLY, max(HEADS + LAG_X, 8 + LAG_Z), step, 0)

    def w_arrive(c, _):
        s_copy(c).wait_recv()
        return 0

    lax.fori_loop(0, HEADS, w_arrive, 0)
    m_copy.wait_recv()

    def project(slots, width):
        into = total.at[:, pl.ds(0, width)]
        into[...] = jnp.zeros((4 * FEAT, width), F32)

        def add(u, _):
            term = None
            for s in range(2):
                k = 2 * u + s
                if slots == (3,):
                    f_copy(k).wait_recv()
            for s in range(2):
                k = 2 * u + s
                rhs = jnp.concatenate([gathered[n, k] for n in slots], axis=0)
                part = lax.dot_general(
                    wt[shifted(k, -1)], rhs, (((1,), (1,)), ((), ())), preferred_element_type=F32
                )
                term = part if term is None else term + part
            into[...] += term
            return 0

        lax.fori_loop(0, 8, add, 0)

    places = (x, lax.rem(x + 3, 4), lax.rem(x + 1, 4), lax.rem(x + 2, 4))

    def o_copy(n, slot):
        row = places[slot] * 4 + low
        return copy_to(
            ostage.at[n, slot], out_ref.at[row], o_send.at[n, slot], o_recv.at[n, slot], mates[n], head
        )

    def o_own(slot):
        return pltpu.make_async_copy(ostage.at[0, slot], out_ref.at[places[slot] * 4 + low], o_send.at[0, slot])

    def o_arrival(n, slot):
        row = places[slot] * 4 + lax.rem(mates[n], 4)
        return copy_to(
            ostage.at[n, slot], out_ref.at[row], o_send.at[n, slot], o_recv.at[n, slot], mates[n], head
        )

    def emit(slots):
        for n in (2, 3, 1, 0):
            for at, slot in enumerate(slots):
                ostage[n, slot] = total[n * FEAT : (n + 1) * FEAT, at * BLK : (at + 1) * BLK].astype(BF16)
                if n:
                    o_copy(n, slot).start()
                else:
                    o_own(slot).start()

    for slots in ((0,), (1, 2), (3,)):
        project(slots, len(slots) * BLK)
        emit(slots)

    for slot in range(4):
        for n in range(1, 4):
            o_arrival(n, slot).wait_recv()
            o_copy(n, slot).wait_send()
        o_own(slot).wait()

    def sent(k, _):
        @pl.when(k > 0)
        def _():
            a_copy(k).wait_send()
        x_copy(0, k).wait_send()
        x_copy(1, k).wait_send()
        f_copy(k).wait_send()
        s_copy(k).wait_send()
        @pl.when(k < 8)
        def _():
            w_copy(k).wait_send()
            z_copy(k, odd).wait_send()
        return 0

    lax.fori_loop(0, HEADS, sent, 0)
    m_copy.wait_send()


def body(queries, keys, values, doc_lengths, out_weight):
    dma = pltpu.SemaphoreType.DMA
    anywhere = pl.BlockSpec(memory_space=pl.ANY)
    mixed = pl.pallas_call(
        kernel,
        out_shape=jax.ShapeDtypeStruct((16, FEAT, BLK), BF16),
        in_specs=[anywhere, anywhere, anywhere, pl.BlockSpec(memory_space=pltpu.SMEM), anywhere],
        out_specs=anywhere,
        scratch_shapes=[
            pltpu.VMEM((SEQ, 2 * HD), BF16),
            pltpu.VMEM((SEQ, HD), BF16),
            pltpu.VMEM((SEQ, HD), BF16),
            pltpu.SMEM((16,), jnp.int32),
            pltpu.VMEM((2 * BLK, 2 * HD), F32),
            pltpu.VMEM((HEADS, BLK, 256), BF16),
            pltpu.VMEM((4, HEADS, BLK, 256), BF16),
            pltpu.VMEM((HEADS, 4 * FEAT, 256), BF16),
            pltpu.VMEM((4 * FEAT, 2 * BLK), F32),
            pltpu.VMEM((4, 4, FEAT, BLK), BF16),
            dma((3,)), dma((HEADS,)),
            dma((HEADS,)), dma((HEADS,)),
            dma((2, HEADS)), dma((2, HEADS)),
            dma((HEADS,)), dma((HEADS,)),
            dma((8,)), dma((8,)),
            dma((8,)), dma((8,)),
            dma((HEADS,)), dma((HEADS,)),
            dma, dma,
            dma((4, 4)), dma((4, 4)),
        ],
        compiler_params=pltpu.CompilerParams(
            collective_id=0, has_side_effects=True, vmem_limit_bytes=56 * 1024 * 1024
        ),
    )(queries, keys, values, doc_lengths, out_weight.T)
    return mixed.transpose(0, 2, 1)


def solution(mesh):
    return jax.shard_map(
        body,
        mesh=mesh,
        in_specs=(P("dp", "head"), P("dp", "head"), P("dp", "head"), P(), P(None, "dp")),
        out_specs=P(None, "head", "dp"),
        check_vma=False,
    )
```

```python
import math

import jax
import jax.numpy as jnp
from jax import lax
from jax.experimental import pallas as pl
from jax.experimental.pallas import tpu as pltpu
from jax.sharding import PartitionSpec as P

HD = 128
BLK = 128
SEQ = 2048
CHUNK = 256
FEAT = 288
HEADS = 16
READY = 6
EARLY = 2
PART = FEAT // 2
RELAY = 4
CHUNKS = 8
FAR_A, BOTH_A, OWN, MATE, FAR_B, BOTH_B = 0, PART, FEAT, 2 * FEAT, 3 * FEAT, 3 * FEAT + PART
LAG_A, LAG_W, LAG_Z, LAG_X = 5, 15, 20, 14
SCALE = 1.0 / 12.0 / 50.0
GAIN = 50.0 * math.log2(math.e)
MESH = pl.DeviceIdType.MESH
F32 = jnp.float32
BF16 = jnp.bfloat16


def kernel(
    q_hbm, k_hbm, v_hbm, doc_ref, w_hbm, out_ref,
    q_ref, k_ref, v_ref, block_doc,
    acc, stage, gathered, wt, total, ostage,
    ld_sem, l_sem, a_send, a_recv, x_send, x_recv, f_send, f_recv,
    w_send, w_recv, z_send, z_recv, s_send, s_recv, m_send, m_recv, o_send, o_recv,
):
    dp, head = lax.axis_index("dp"), lax.axis_index("head")
    x, low = dp // 4, lax.rem(dp, 4)
    z, y_high = head // 2, lax.rem(head, 2)
    odd = lax.rem(z, 2)
    right = lax.rem(x + 1, 4) * 4 + low
    left = lax.rem(x + 3, 4) * 4 + low
    core_mate = dp + 1 - 2 * lax.rem(dp, 2)
    y_mate = dp + 2 - 4 * lax.rem(dp // 2, 2)
    both_mate = core_mate + 2 - 4 * lax.rem(dp // 2, 2)
    head_mate = head + 1 - 2 * y_high
    mates = (dp, core_mate, y_mate, both_mate)

    def copy_to(src, dst, send, recv, to_dp, to_head):
        return pltpu.make_async_remote_copy(
            src_ref=src, dst_ref=dst, send_sem=send, recv_sem=recv,
            device_id={"dp": to_dp, "head": to_head}, device_id_type=MESH,
        )

    def shifted(k, sign):
        far = (k + 2) // 4
        up = jnp.where(lax.rem(k, 2) == 0, far, 8 - far)
        across = jnp.where((far == 0) | (far == 4), lax.rem(k, 2), lax.rem(k // 2 + 1, 2))
        return lax.rem(z + 8 + sign * up, 8) * 2 + lax.rem(y_high + across, 2)

    loads = [
        pltpu.make_async_copy(q_hbm, q_ref, ld_sem.at[0]),
        pltpu.make_async_copy(k_hbm, k_ref, ld_sem.at[1]),
        pltpu.make_async_copy(v_hbm, v_ref, ld_sem.at[2]),
    ]
    for load in loads:
        load.start()

    def w_load(n):
        cols = pl.ds(pl.multiple_of(n * 256, 256), 256)
        return pltpu.make_async_copy(w_hbm.at[:, cols], wt.at[n, pl.ds(OWN, FEAT)], l_sem.at[n])

    def start_load(n, _):
        w_load(n).start()
        return 0

    lax.fori_loop(0, HEADS, start_load, 0)
    barrier = pltpu.get_barrier_semaphore()

    def greet(to_dp, to_head):
        pl.semaphore_signal(barrier, inc=1, device_id={"dp": to_dp, "head": to_head}, device_id_type=MESH)

    def greet_heads(n, _):
        greet(dp, lax.rem(head + n, HEADS))
        return 0

    lax.fori_loop(1, HEADS, greet_heads, 0)
    greet(right, head)
    greet(left, head)
    greet(core_mate, head)
    greet(y_mate, head)
    greet(both_mate, head)
    greet(y_mate, head_mate)

    ends = []
    end = jnp.int32(0)
    for n in range(16):
        end = end + doc_ref[dp, n]
        ends.append(end)

    def number(b, _):
        count = jnp.int32(0)
        for end in ends:
            count = count + jnp.where(end <= b * BLK, 1, 0).astype(jnp.int32)
        block_doc[b] = count
        return 0

    lax.fori_loop(0, 16, number, 0)
    for load in loads:
        load.wait()

    differences = lax.rem(lax.broadcasted_iota(jnp.int32, (2 * BLK, CHUNK), 0), BLK) - lax.broadcasted_iota(
        jnp.int32, (2 * BLK, CHUNK), 1
    )

    def tile(q_two, block, chunk, diagonal):
        cols = pl.ds(pl.multiple_of(chunk * CHUNK, CHUNK), CHUNK)
        raw = lax.dot_general(q_two, k_ref[cols, :], (((1,), (1,)), ((), ())), preferred_element_type=F32)
        weight = jnp.exp2(jnp.tanh(raw * SCALE) * GAIN)
        if diagonal:
            weight = jnp.where(differences >= chunk * CHUNK - block * BLK, weight, 0.0)
        own = block_doc[block]
        live = []
        for n in range(2):
            on = block_doc[2 * chunk + n] == own
            if not diagonal:
                on = jnp.logical_and(on, chunk < block // 2)
            live.append(jnp.full((BLK, HD), jnp.where(on, 1.0, 0.0).astype(F32), F32).astype(BF16))
        live = jnp.concatenate(live, axis=0)
        value_two = jnp.concatenate([v_ref[cols, :] * live, live], axis=1)
        return jnp.dot(weight.astype(BF16), value_two, preferred_element_type=F32)

    def attend(k, block, into):
        rows = pl.ds(pl.multiple_of(block * BLK, BLK), BLK)

        def tiles(others):
            q_two = jnp.concatenate([q_ref[rows, 0:HD], q_ref[rows, HD : 2 * HD]], axis=0)
            both = tile(q_two, block, block // 2, True)
            for n in range(others):
                both = both + tile(q_two, block, n, False)
            acc[...] = both

        pl.when(block < 8)(lambda: tiles(3))
        pl.when(block >= 8)(lambda: tiles(7))
        both = acc[...]
        result = (both[:, 0:HD] / both[:, HD : 2 * HD]).astype(BF16)
        into[...] = jnp.concatenate([result[0:BLK], result[BLK : 2 * BLK]], axis=1)

    def a_copy(k):
        return copy_to(stage.at[k], gathered.at[0, k], a_send.at[k], a_recv.at[k], dp, shifted(k, 1))

    def x_copy(way, k):
        return copy_to(
            gathered.at[0, k], gathered.at[1 + way, k], x_send.at[way, k], x_recv.at[way, k],
            right if way == 0 else left, head,
        )

    def f_copy(k):
        way = lax.rem(k, 2)
        return copy_to(
            gathered.at[1 + way, k], gathered.at[3, k], f_send.at[k], f_recv.at[k],
            jnp.where(way == 0, right, left), head,
        )

    def piece(c, row, count):
        return wt.at[pl.ds(2 * c, 2), pl.ds(row, count)]

    def w_chunk(n):
        return jnp.where(n < RELAY, 2 * n + odd, n - RELAY)

    def w_copy(n, part):
        c = w_chunk(n)
        return copy_to(
            piece(c, OWN + part * PART, PART), piece(c, FAR_B if part else FAR_A, PART), w_send.at[n], w_recv.at[n],
            y_mate, jnp.where(lax.rem(n, 2) == 0, head, head_mate),
        )

    def z_copy(n, parity):
        c = 2 * n + parity
        up = jnp.where(lax.rem(n // 2, 2) == 0, 1, 7)
        return copy_to(
            piece(c, FAR_A, PART), piece(c, FAR_A, PART), z_send.at[n], z_recv.at[n],
            dp, lax.rem(z + up, 8) * 2 + y_high,
        )

    def s_copy(c, part):
        return copy_to(
            piece(c, FAR_B if part else FAR_A, PART), piece(c, BOTH_B if part else BOTH_A, PART),
            s_send.at[part, c], s_recv.at[part, c], core_mate, head,
        )

    m_copy = copy_to(
        wt.at[:, pl.ds(OWN, FEAT)], wt.at[:, pl.ds(MATE, FEAT)], m_send, m_recv, core_mate, head
    )

    attend(0, head, gathered.at[0, 0])

    def early(k, _):
        attend(k, shifted(k, 1), stage.at[k])
        return 0

    lax.fori_loop(1, EARLY, early, 0)

    def end_load(n, _):
        w_load(n).wait()
        return 0

    lax.fori_loop(0, HEADS, end_load, 0)
    total[OWN : OWN + 2 * FEAT, 0 : 3 * BLK] = jnp.zeros((2 * FEAT, 3 * BLK), F32)
    pl.semaphore_wait(barrier, 21)

    def early_send(k, _):
        a_copy(k).start()
        return 0

    lax.fori_loop(1, EARLY, early_send, 0)

    def send_w(n, _):
        w_copy(n, 0).start()
        return 0

    lax.fori_loop(0, RELAY, send_w, 0)
    m_copy.start()

    def step(t, _):
        @pl.when(t < HEADS)
        def _():
            attend(t, shifted(t, 1), stage.at[t])
            a_copy(t).start()

        def during(lag, count, act):
            k = t - lag
            pl.when(jnp.logical_and(k >= 0, k < count))(lambda: act(k))

        def pass_own(k):
            @pl.when(k > 0)
            def _():
                a_copy(k).wait_recv()
            x_copy(0, k).start()
            x_copy(1, k).start()

        def pass_w(n):
            w_copy(n, 0).wait_recv()
            w_copy(RELAY + 2 * n, 1).start()
            w_copy(RELAY + 2 * n + 1, 1).start()
            z_copy(n, odd).start()
            s_copy(2 * n + odd, 0).start()

        def pass_z(n):
            z_copy(n, 1 - odd).wait_recv()
            s_copy(2 * n + 1 - odd, 0).start()

        def pass_far(k):
            x_copy(0, k).wait_recv()
            x_copy(1, k).wait_recv()
            f_copy(k).start()
            pl.when(k == 0)(lambda: m_copy.wait_recv())
            rhs = jnp.concatenate([gathered[n, k] for n in range(3)], axis=0)
            total[OWN : OWN + 2 * FEAT, 0 : 3 * BLK] += lax.dot_general(
                wt[shifted(k, -1), OWN : OWN + 2 * FEAT, :], rhs, (((1,), (1,)), ((), ())),
                preferred_element_type=F32,
            )

        during(LAG_A, HEADS, pass_own)
        during(LAG_W, RELAY, pass_w)
        during(LAG_Z, RELAY, pass_z)
        during(LAG_X, HEADS, pass_far)
        return 0

    lax.fori_loop(EARLY, max(HEADS + LAG_X, RELAY + LAG_Z), step, 0)

    def w_direct(n, _):
        w_copy(n, 1).wait_recv()
        s_copy(w_chunk(n), 1).start()
        return 0

    def w_arrive(part):
        def one(c, _):
            s_copy(c, part).wait_recv()
            return 0

        lax.fori_loop(0, CHUNKS, one, 0)

    def project(slots, first, count, start=0, stop=8, arriving=False):
        into = total.at[pl.ds(first, count), pl.ds(slots[0] * BLK, len(slots) * BLK)]
        if start == 0:
            into[...] = jnp.zeros((count, len(slots) * BLK), F32)

        def add(u, _):
            if arriving:
                f_copy(2 * u).wait_recv()
                f_copy(2 * u + 1).wait_recv()
            term = None
            for s in range(2):
                k = 2 * u + s
                rhs = jnp.concatenate([gathered[n, k] for n in slots], axis=0)
                part = lax.dot_general(
                    wt[shifted(k, -1), first : first + count, :], rhs, (((1,), (1,)), ((), ())),
                    preferred_element_type=F32,
                )
                term = part if term is None else term + part
            into[...] += term
            return 0

        lax.fori_loop(start, stop, add, 0)

    places = (x, lax.rem(x + 3, 4), lax.rem(x + 1, 4), lax.rem(x + 2, 4))

    def o_copy(n, slot, part, row_of=dp):
        row = places[slot] * 4 + lax.rem(row_of, 4)
        rows = pl.ds(0, FEAT) if n == 1 else pl.ds(part * PART, PART)
        return copy_to(
            ostage.at[n, slot, rows], out_ref.at[row, rows], o_send.at[n, slot, part], o_recv.at[n, slot, part],
            mates[n], head,
        )

    def o_own(slot):
        return pltpu.make_async_copy(ostage.at[0, slot], out_ref.at[places[slot] * 4 + low], o_send.at[0, slot, 0])

    def result(slot, row, count):
        return total[row : row + count, slot * BLK : (slot + 1) * BLK].astype(BF16)

    def emit_part(slots, part):
        for slot in slots:
            for n in (2, 3):
                row = (FAR_B if part else FAR_A) + (n - 2) * PART
                ostage[n, slot, part * PART : (part + 1) * PART] = result(slot, row, PART)
                o_copy(n, slot, part).start()

    def emit_chip(slots):
        for slot in slots:
            ostage[1, slot] = result(slot, MATE, FEAT)
            o_copy(1, slot, 0).start()
            ostage[0, slot] = result(slot, OWN, FEAT)
            o_own(slot).start()

    near, last = (0, 1, 2), (3,)
    w_arrive(0)
    project(near, FAR_A, FEAT)
    emit_part(near, 0)
    lax.fori_loop(RELAY, RELAY + CHUNKS, w_direct, 0)
    emit_chip(near)
    project(last, FAR_A, 3 * FEAT, 0, READY, arriving=True)
    w_arrive(1)
    project(near, FAR_B, FEAT)
    emit_part(near, 1)
    project(last, FAR_B, FEAT, 0, READY)
    project(last, FAR_A, 4 * FEAT, READY, 8, arriving=True)
    emit_part(last, 0)
    emit_part(last, 1)
    emit_chip(last)

    for slot in range(4):
        for n, part in ((1, 0), (2, 0), (3, 0), (2, 1), (3, 1)):
            o_copy(n, slot, part, mates[n]).wait_recv()
            o_copy(n, slot, part).wait_send()
        o_own(slot).wait()

    def sent(k, _):
        @pl.when(k > 0)
        def _():
            a_copy(k).wait_send()
        x_copy(0, k).wait_send()
        x_copy(1, k).wait_send()
        f_copy(k).wait_send()
        pl.when(k < CHUNKS)(lambda: s_copy(k, 0).wait_send())
        pl.when(k < CHUNKS)(lambda: s_copy(k, 1).wait_send())
        pl.when(k < RELAY)(lambda: w_copy(k, 0).wait_send())
        pl.when(jnp.logical_and(k >= RELAY, k < RELAY + CHUNKS))(lambda: w_copy(k, 1).wait_send())
        pl.when(k < RELAY)(lambda: z_copy(k, odd).wait_send())
        return 0

    lax.fori_loop(0, HEADS, sent, 0)
    m_copy.wait_send()


def body(queries, keys, values, doc_lengths, out_weight):
    dma = pltpu.SemaphoreType.DMA
    anywhere = pl.BlockSpec(memory_space=pl.ANY)
    mixed = pl.pallas_call(
        kernel,
        out_shape=jax.ShapeDtypeStruct((16, FEAT, BLK), BF16),
        in_specs=[anywhere, anywhere, anywhere, pl.BlockSpec(memory_space=pltpu.SMEM), anywhere],
        out_specs=anywhere,
        scratch_shapes=[
            pltpu.VMEM((SEQ, 2 * HD), BF16),
            pltpu.VMEM((SEQ, HD), BF16),
            pltpu.VMEM((SEQ, HD), BF16),
            pltpu.SMEM((16,), jnp.int32),
            pltpu.VMEM((2 * BLK, 2 * HD), F32),
            pltpu.VMEM((HEADS, BLK, 256), BF16),
            pltpu.VMEM((4, HEADS, BLK, 256), BF16),
            pltpu.VMEM((HEADS, 4 * FEAT, 256), BF16),
            pltpu.VMEM((4 * FEAT, 4 * BLK), F32),
            pltpu.VMEM((4, 4, FEAT, BLK), BF16),
            dma((3,)), dma((HEADS,)),
            dma((HEADS,)), dma((HEADS,)),
            dma((2, HEADS)), dma((2, HEADS)),
            dma((HEADS,)), dma((HEADS,)),
            dma((RELAY + CHUNKS,)), dma((RELAY + CHUNKS,)),
            dma((RELAY,)), dma((RELAY,)),
            dma((2, CHUNKS)), dma((2, CHUNKS)),
            dma, dma,
            dma((4, 4, 2)), dma((4, 4, 2)),
        ],
        compiler_params=pltpu.CompilerParams(
            collective_id=0, has_side_effects=True, vmem_limit_bytes=56 * 1024 * 1024
        ),
    )(queries, keys, values, doc_lengths, out_weight.T)
    return mixed.transpose(0, 2, 1)


def solution(mesh):
    return jax.shard_map(
        body,
        mesh=mesh,
        in_specs=(P("dp", "head"), P("dp", "head"), P("dp", "head"), P(), P(None, "dp")),
        out_specs=P(None, "head", "dp"),
        check_vma=False,
    )
```

```python
import math

import jax
import jax.numpy as jnp
from jax import lax
from jax.experimental import pallas as pl
from jax.experimental.pallas import tpu as pltpu
from jax.sharding import PartitionSpec as P

HD = 128
BLK = 128
SEQ = 2048
CHUNK = 256
FEAT = 288
HEADS = 16
READY = 6
EARLY = 2
PART = FEAT // 2
RELAY = 4
CHUNKS = 8
FAR_A, BOTH_A, OWN, MATE, FAR_B, BOTH_B = 0, PART, FEAT, 2 * FEAT, 3 * FEAT, 3 * FEAT + PART
LAG_A, LAG_W, LAG_Z, LAG_X = 5, 16, 23, 14
SCALE = 1.0 / 12.0 / 50.0
GAIN = 50.0 * math.log2(math.e)
MESH = pl.DeviceIdType.MESH
F32 = jnp.float32
BF16 = jnp.bfloat16


def kernel(
    q_hbm, k_hbm, v_hbm, doc_ref, w_hbm, out_ref,
    q_ref, k_ref, v_ref, block_doc,
    acc, stage, gathered, wt, total, ostage,
    ld_sem, l_sem, a_send, a_recv, x_send, x_recv, f_send, f_recv,
    w_send, w_recv, z_send, z_recv, s_send, s_recv, m_send, m_recv, o_send, o_recv,
):
    dp, head = lax.axis_index("dp"), lax.axis_index("head")
    x, low = dp // 4, lax.rem(dp, 4)
    z, y_high = head // 2, lax.rem(head, 2)
    odd = lax.rem(z, 2)
    right = lax.rem(x + 1, 4) * 4 + low
    left = lax.rem(x + 3, 4) * 4 + low
    core_mate = dp + 1 - 2 * lax.rem(dp, 2)
    y_mate = dp + 2 - 4 * lax.rem(dp // 2, 2)
    both_mate = core_mate + 2 - 4 * lax.rem(dp // 2, 2)
    head_mate = head + 1 - 2 * y_high
    mates = (dp, core_mate, y_mate, both_mate)

    def copy_to(src, dst, send, recv, to_dp, to_head):
        return pltpu.make_async_remote_copy(
            src_ref=src, dst_ref=dst, send_sem=send, recv_sem=recv,
            device_id={"dp": to_dp, "head": to_head}, device_id_type=MESH,
        )

    def shifted(k, sign):
        far = (k + 2) // 4
        up = jnp.where(lax.rem(k, 2) == 0, far, 8 - far)
        across = jnp.where((far == 0) | (far == 4), lax.rem(k, 2), lax.rem(k // 2 + 1, 2))
        return lax.rem(z + 8 + sign * up, 8) * 2 + lax.rem(y_high + across, 2)

    loads = [
        pltpu.make_async_copy(q_hbm, q_ref, ld_sem.at[0]),
        pltpu.make_async_copy(k_hbm, k_ref, ld_sem.at[1]),
        pltpu.make_async_copy(v_hbm, v_ref, ld_sem.at[2]),
    ]
    for load in loads:
        load.start()

    def w_load(n):
        cols = pl.ds(pl.multiple_of(n * 256, 256), 256)
        return pltpu.make_async_copy(w_hbm.at[:, cols], wt.at[n, pl.ds(OWN, FEAT)], l_sem.at[n])

    def start_load(n, _):
        w_load(n).start()
        return 0

    lax.fori_loop(0, HEADS, start_load, 0)
    barrier = pltpu.get_barrier_semaphore()

    def greet(to_dp, to_head):
        pl.semaphore_signal(barrier, inc=1, device_id={"dp": to_dp, "head": to_head}, device_id_type=MESH)

    def greet_heads(n, _):
        greet(dp, lax.rem(head + n, HEADS))
        return 0

    lax.fori_loop(1, HEADS, greet_heads, 0)
    greet(right, head)
    greet(left, head)
    greet(core_mate, head)
    greet(y_mate, head)
    greet(both_mate, head)
    greet(y_mate, head_mate)

    ends = []
    end = jnp.int32(0)
    for n in range(16):
        end = end + doc_ref[dp, n]
        ends.append(end)

    def number(b, _):
        count = jnp.int32(0)
        for end in ends:
            count = count + jnp.where(end <= b * BLK, 1, 0).astype(jnp.int32)
        block_doc[b] = count
        return 0

    lax.fori_loop(0, 16, number, 0)
    for load in loads:
        load.wait()

    differences = lax.rem(lax.broadcasted_iota(jnp.int32, (2 * BLK, CHUNK), 0), BLK) - lax.broadcasted_iota(
        jnp.int32, (2 * BLK, CHUNK), 1
    )

    def tile(q_two, block, chunk, diagonal):
        cols = pl.ds(pl.multiple_of(chunk * CHUNK, CHUNK), CHUNK)
        raw = lax.dot_general(q_two, k_ref[cols, :], (((1,), (1,)), ((), ())), preferred_element_type=F32)
        weight = jnp.exp2(jnp.tanh(raw * SCALE) * GAIN)
        if diagonal:
            weight = jnp.where(differences >= chunk * CHUNK - block * BLK, weight, 0.0)
        own = block_doc[block]
        live = []
        for n in range(2):
            on = block_doc[2 * chunk + n] == own
            if not diagonal:
                on = jnp.logical_and(on, chunk < block // 2)
            live.append(jnp.full((BLK, HD), jnp.where(on, 1.0, 0.0).astype(F32), F32).astype(BF16))
        live = jnp.concatenate(live, axis=0)
        value_two = jnp.concatenate([v_ref[cols, :] * live, live], axis=1)
        return jnp.dot(weight.astype(BF16), value_two, preferred_element_type=F32)

    def attend(k, block, into):
        rows = pl.ds(pl.multiple_of(block * BLK, BLK), BLK)

        def tiles(others):
            q_two = jnp.concatenate([q_ref[rows, 0:HD], q_ref[rows, HD : 2 * HD]], axis=0)
            both = tile(q_two, block, block // 2, True)
            for n in range(others):
                both = both + tile(q_two, block, n, False)
            acc[...] = both

        for level in range(4):
            pl.when(block // 4 == level)(lambda: tiles(2 * level + 1))
        both = acc[...]
        result = (both[:, 0:HD] / both[:, HD : 2 * HD]).astype(BF16)
        into[...] = jnp.concatenate([result[0:BLK], result[BLK : 2 * BLK]], axis=1)

    def a_copy(k):
        return copy_to(stage.at[k], gathered.at[0, k], a_send.at[k], a_recv.at[k], dp, shifted(k, 1))

    def x_copy(way, k):
        return copy_to(
            gathered.at[0, k], gathered.at[1 + way, k], x_send.at[way, k], x_recv.at[way, k],
            right if way == 0 else left, head,
        )

    def f_copy(k):
        way = lax.rem(k, 2)
        return copy_to(
            gathered.at[1 + way, k], gathered.at[3, k], f_send.at[k], f_recv.at[k],
            jnp.where(way == 0, right, left), head,
        )

    def piece(c, row, count):
        return wt.at[pl.ds(2 * c, 2), pl.ds(row, count)]

    def w_chunk(n):
        return jnp.where(n < RELAY, 2 * n + odd, n - RELAY)

    def w_copy(n, part):
        c = w_chunk(n)
        return copy_to(
            piece(c, OWN + part * PART, PART), piece(c, FAR_B if part else FAR_A, PART), w_send.at[n], w_recv.at[n],
            y_mate, jnp.where(lax.rem(n, 2) == 0, head, head_mate),
        )

    def z_copy(n, parity):
        c = 2 * n + parity
        up = jnp.where(lax.rem(n // 2, 2) == 0, 1, 7)
        return copy_to(
            piece(c, FAR_A, PART), piece(c, FAR_A, PART), z_send.at[n], z_recv.at[n],
            dp, lax.rem(z + up, 8) * 2 + y_high,
        )

    def s_copy(c, part):
        return copy_to(
            piece(c, FAR_B if part else FAR_A, PART), piece(c, BOTH_B if part else BOTH_A, PART),
            s_send.at[part, c], s_recv.at[part, c], core_mate, head,
        )

    m_copy = copy_to(
        wt.at[:, pl.ds(OWN, FEAT)], wt.at[:, pl.ds(MATE, FEAT)], m_send, m_recv, core_mate, head
    )

    attend(0, head, gathered.at[0, 0])

    def early(k, _):
        attend(k, shifted(k, 1), stage.at[k])
        return 0

    lax.fori_loop(1, EARLY, early, 0)

    def end_load(n, _):
        w_load(n).wait()
        return 0

    lax.fori_loop(0, HEADS, end_load, 0)
    total[OWN : OWN + 2 * FEAT, 0 : 3 * BLK] = jnp.zeros((2 * FEAT, 3 * BLK), F32)
    pl.semaphore_wait(barrier, 21)

    def early_send(k, _):
        a_copy(k).start()
        return 0

    lax.fori_loop(1, EARLY, early_send, 0)
    x_copy(0, 0).start()
    x_copy(1, 0).start()

    def send_w(n, _):
        w_copy(n, 0).start()
        return 0

    lax.fori_loop(0, RELAY, send_w, 0)
    m_copy.start()

    def step(t, _):
        @pl.when(t < HEADS)
        def _():
            attend(t, shifted(t, 1), stage.at[t])
            a_copy(t).start()

        def during(lag, count, act):
            k = t - lag
            pl.when(jnp.logical_and(k >= 0, k < count))(lambda: act(k))

        def pass_own(k):
            @pl.when(k > 0)
            def _():
                a_copy(k).wait_recv()
            @pl.when(k > 0)
            def _():
                x_copy(0, k).start()
                x_copy(1, k).start()

        def pass_w(n):
            w_copy(n, 0).wait_recv()
            w_copy(RELAY + 2 * n, 1).start()
            w_copy(RELAY + 2 * n + 1, 1).start()
            z_copy(n, odd).start()
            s_copy(2 * n + odd, 0).start()

        def pass_z(n):
            z_copy(n, 1 - odd).wait_recv()
            s_copy(2 * n + 1 - odd, 0).start()

        def pass_far(k):
            x_copy(0, k).wait_recv()
            x_copy(1, k).wait_recv()
            f_copy(k).start()
            pl.when(k == 0)(lambda: m_copy.wait_recv())
            rhs = jnp.concatenate([gathered[n, k] for n in range(3)], axis=0)
            total[OWN : OWN + 2 * FEAT, 0 : 3 * BLK] += lax.dot_general(
                wt[shifted(k, -1), OWN : OWN + 2 * FEAT, :], rhs, (((1,), (1,)), ((), ())),
                preferred_element_type=F32,
            )

        during(LAG_A, HEADS, pass_own)
        during(LAG_W, RELAY, pass_w)
        during(LAG_Z, RELAY, pass_z)
        during(LAG_X, HEADS, pass_far)
        return 0

    lax.fori_loop(EARLY, max(HEADS + LAG_X, RELAY + LAG_Z), step, 0)

    def w_direct(n, _):
        w_copy(n, 1).wait_recv()
        s_copy(w_chunk(n), 1).start()
        return 0

    def w_arrive(part):
        def one(c, _):
            s_copy(c, part).wait_recv()
            return 0

        lax.fori_loop(0, CHUNKS, one, 0)

    def project(slots, first, count, start=0, stop=8, arriving=False):
        into = total.at[pl.ds(first, count), pl.ds(slots[0] * BLK, len(slots) * BLK)]
        if start == 0:
            into[...] = jnp.zeros((count, len(slots) * BLK), F32)

        def add(u, _):
            if arriving:
                f_copy(2 * u).wait_recv()
                f_copy(2 * u + 1).wait_recv()
            term = None
            for s in range(2):
                k = 2 * u + s
                rhs = jnp.concatenate([gathered[n, k] for n in slots], axis=0)
                part = lax.dot_general(
                    wt[shifted(k, -1), first : first + count, :], rhs, (((1,), (1,)), ((), ())),
                    preferred_element_type=F32,
                )
                term = part if term is None else term + part
            into[...] += term
            return 0

        lax.fori_loop(start, stop, add, 0)

    places = (x, lax.rem(x + 3, 4), lax.rem(x + 1, 4), lax.rem(x + 2, 4))

    def o_copy(n, slot, part, row_of=dp):
        row = places[slot] * 4 + lax.rem(row_of, 4)
        rows = pl.ds(0, FEAT) if n == 1 else pl.ds(part * PART, PART)
        return copy_to(
            ostage.at[n, slot, rows], out_ref.at[row, rows], o_send.at[n, slot, part], o_recv.at[n, slot, part],
            mates[n], head,
        )

    def o_own(slot):
        return pltpu.make_async_copy(ostage.at[0, slot], out_ref.at[places[slot] * 4 + low], o_send.at[0, slot, 0])

    def result(slot, row, count):
        return total[row : row + count, slot * BLK : (slot + 1) * BLK].astype(BF16)

    def emit_part(slots, part):
        for slot in slots:
            for n in (2, 3):
                row = (FAR_B if part else FAR_A) + (n - 2) * PART
                ostage[n, slot, part * PART : (part + 1) * PART] = result(slot, row, PART)
                o_copy(n, slot, part).start()

    def emit_chip(slots):
        for slot in slots:
            ostage[1, slot] = result(slot, MATE, FEAT)
            o_copy(1, slot, 0).start()
            ostage[0, slot] = result(slot, OWN, FEAT)
            o_own(slot).start()

    near, last = (0, 1, 2), (3,)
    w_arrive(0)
    project(near, FAR_A, FEAT)
    emit_part(near, 0)
    lax.fori_loop(RELAY, RELAY + CHUNKS, w_direct, 0)
    emit_chip(near)
    project(last, FAR_A, 3 * FEAT, 0, READY, arriving=True)
    w_arrive(1)
    project(near, FAR_B, FEAT)
    emit_part(near, 1)
    project(last, FAR_B, FEAT, 0, READY)
    project(last, FAR_A, 4 * FEAT, READY, 8, arriving=True)
    emit_part(last, 0)
    emit_part(last, 1)
    emit_chip(last)

    for slot in range(4):
        for n, part in ((1, 0), (2, 0), (3, 0), (2, 1), (3, 1)):
            o_copy(n, slot, part, mates[n]).wait_recv()
            o_copy(n, slot, part).wait_send()
        o_own(slot).wait()

    def sent(k, _):
        @pl.when(k > 0)
        def _():
            a_copy(k).wait_send()
        x_copy(0, k).wait_send()
        x_copy(1, k).wait_send()
        f_copy(k).wait_send()
        pl.when(k < CHUNKS)(lambda: s_copy(k, 0).wait_send())
        pl.when(k < CHUNKS)(lambda: s_copy(k, 1).wait_send())
        pl.when(k < RELAY)(lambda: w_copy(k, 0).wait_send())
        pl.when(jnp.logical_and(k >= RELAY, k < RELAY + CHUNKS))(lambda: w_copy(k, 1).wait_send())
        pl.when(k < RELAY)(lambda: z_copy(k, odd).wait_send())
        return 0

    lax.fori_loop(0, HEADS, sent, 0)
    m_copy.wait_send()


def body(queries, keys, values, doc_lengths, out_weight):
    dma = pltpu.SemaphoreType.DMA
    anywhere = pl.BlockSpec(memory_space=pl.ANY)
    mixed = pl.pallas_call(
        kernel,
        out_shape=jax.ShapeDtypeStruct((16, FEAT, BLK), BF16),
        in_specs=[anywhere, anywhere, anywhere, pl.BlockSpec(memory_space=pltpu.SMEM), anywhere],
        out_specs=anywhere,
        scratch_shapes=[
            pltpu.VMEM((SEQ, 2 * HD), BF16),
            pltpu.VMEM((SEQ, HD), BF16),
            pltpu.VMEM((SEQ, HD), BF16),
            pltpu.SMEM((16,), jnp.int32),
            pltpu.VMEM((2 * BLK, 2 * HD), F32),
            pltpu.VMEM((HEADS, BLK, 256), BF16),
            pltpu.VMEM((4, HEADS, BLK, 256), BF16),
            pltpu.VMEM((HEADS, 4 * FEAT, 256), BF16),
            pltpu.VMEM((4 * FEAT, 4 * BLK), F32),
            pltpu.VMEM((4, 4, FEAT, BLK), BF16),
            dma((3,)), dma((HEADS,)),
            dma((HEADS,)), dma((HEADS,)),
            dma((2, HEADS)), dma((2, HEADS)),
            dma((HEADS,)), dma((HEADS,)),
            dma((RELAY + CHUNKS,)), dma((RELAY + CHUNKS,)),
            dma((RELAY,)), dma((RELAY,)),
            dma((2, CHUNKS)), dma((2, CHUNKS)),
            dma, dma,
            dma((4, 4, 2)), dma((4, 4, 2)),
        ],
        compiler_params=pltpu.CompilerParams(
            collective_id=0, has_side_effects=True, vmem_limit_bytes=56 * 1024 * 1024
        ),
    )(queries, keys, values, doc_lengths, out_weight.T)
    return mixed.transpose(0, 2, 1)


def solution(mesh):
    return jax.shard_map(
        body,
        mesh=mesh,
        in_specs=(P("dp", "head"), P("dp", "head"), P("dp", "head"), P(), P(None, "dp")),
        out_specs=P(None, "head", "dp"),
        check_vma=False,
    )
```
